128 devices in a mesh: node: 8 (over y, core), local: 16 (over z, x).
Axes of the slice: x: 4, y: 4, z: 4, core: 2. Of those that a mesh axis runs over, the one named last changes fastest.
Arguments:
- tokens: bfloat16 [98304, 8192], P(('node', 'local')), may hold values from -24 to 24
- out_grads: bfloat16 [98304, 1024], P(('node', 'local')), may hold values from -0.21582031 to 0.21582031
- master: float32 [8192, 1024], P(('node', 'local')), may hold values from -6 to 6
- moment: float32 [8192, 1024], P(('node', 'local')), may hold values from -18 to 18
- second: float32 [8192, 1024], P(('node', 'local')), may hold values from 0.1 to 100
Outputs:
- new_master: float32 [8192, 1024], P(('node', 'local'))
- new_moment: float32 [8192, 1024], P(('node', 'local'))
- new_second: float32 [8192, 1024], P(('node', 'local'))
- weight_copy: bfloat16 [8, 1024, 1024], P(None, 'local')
The draws below stay inside these ranges and needn't reach their ends.
All inputs are finite; a program needn't handle non-finite values. Where the reference program divides by a largest or mean magnitude, that divisor is 1e-20 or more.
Results may differ from the reference program's by a relative error of at most 0.001.
Values may be sent and summed in bfloat16 or wider, within the bound.
No kernel may reach another device: no remote copies, remote signals or barrier semaphores. Data moves between devices by JAX's collectives and lax.ppermute only.
A program may use at most 256 MiB of HBM per device.

```python
import math
import jax
import jax.numpy as jnp
from jax import lax

D = 8192
KV = 1024
QBLOCK = 128
TOK_DEV = 768
TOKENS = 98304
N_NODE = 8
N_LOCAL = 16


def raised(drawn, rng, source, target, blocks, factor):
    def block_of(axis_at):
        return (jnp.arange(drawn.shape[axis_at]) // (drawn.shape[axis_at] // blocks)).reshape((-1,) + (1,) * (drawn.ndim - 1 - axis_at))

    near = jax.random.permutation(rng, blocks)[block_of(target)]
    second = (block_of(target) + blocks // 2) % blocks
    return jnp.where((block_of(source) == near) | (block_of(source) == second), factor * drawn, drawn)


def level_of(own_key, dims, shards, smallest, top_value):
    def one(position, parts):
        steps = jax.random.uniform(jax.random.fold_in(jax.random.fold_in(own_key, 6), position), (parts,), jnp.float32, smallest / len(shards), top_value / len(shards))
        return jnp.repeat(jnp.exp(steps), dims[position] // parts).reshape((-1,) + (1,) * (len(dims) - position - 1))

    factor_of = one(*shards[0])
    for cut in shards[1:]:
        factor_of = factor_of * one(*cut)
    return factor_of


def normal_values(own_key, dims, scale, limit, split=(), dtype=jnp.bfloat16):
    factor_of = level_of(own_key, dims, split, -0.22, 0.18) if split else 1.0
    entries = jax.random.normal(own_key, dims, jnp.float32) * scale * factor_of
    return jnp.minimum(jnp.maximum(entries, -limit), limit).astype(dtype)


def bell_draw_with(stream_key, extent, scale, reach, shards, heavy, kind=jnp.bfloat16):
    entries = scale * jax.random.normal(stream_key, extent, jnp.float32)
    if shards:
        entries = entries * level_of(stream_key, extent, shards, -0.22, 0.18)
    return jnp.clip(raised(entries, jax.random.fold_in(stream_key, 3), *heavy), -reach, reach).astype(kind)


def setup_inputs(seed: int = 0) -> dict:
    seeds = jax.random.split(jax.random.key(seed), 6)
    tokens = bell_draw_with(seeds[0], (TOKENS, D), 1.0, 24.0, ((0, 128),), (0, 1, 128, 5.5))
    out_grads = normal_values(seeds[1], (TOKENS, KV), (TOK_DEV ** -0.5), 0.21582031, ((0, 128),))
    master = normal_values(seeds[2], (D, KV), 1.0, 6.0, ((0, 128),), jnp.float32)
    moment = normal_values(seeds[3], (D, KV), 3.0, 18.0, ((0, 128),), jnp.float32)
    second = jnp.clip(jnp.exp(math.log(100.0) - 6.9077553 * jax.random.uniform(seeds[4], (D, KV), jnp.float32) ** level_of(seeds[4], (D, KV), ((0, 128),), -0.2, 0.2)), 0.1, 100.0)
    return dict(tokens=tokens, out_grads=out_grads, master=master, moment=moment, second=second)


def quantize(values):
    shape = values.shape
    blocks = values.reshape(shape[:-1] + (shape[-1] // QBLOCK, QBLOCK))
    scale = (lax.optimization_barrier(jnp.max(jnp.abs(blocks), axis=-1)) + 1e-06).astype(jnp.bfloat16)
    codes = (blocks / scale.astype(jnp.float32)[..., None]).astype(jnp.bfloat16)
    return (codes.reshape(shape), scale)

def restore(codes, scale):
    shape = codes.shape
    blocks = codes.astype(jnp.float32).reshape(shape[:-1] + (shape[-1] // QBLOCK, QBLOCK))
    return (blocks * scale.astype(jnp.float32)[..., None]).reshape(shape)

def reference(tokens, out_grads, master, moment, second):
    inputs = tokens.reshape(N_NODE, N_LOCAL, TOK_DEV, D)
    outputs = out_grads.reshape(N_NODE, N_LOCAL, TOK_DEV, KV)

    def node_step(total, pair):

        def local_step(accum, inner):
            grad_block = jnp.dot(inner[0].T, inner[1], preferred_element_type=jnp.float32)
            codes, scale = quantize(grad_block)
            return (accum + restore(codes, scale), None)
        partial_sum, _ = lax.scan(local_step, jnp.zeros((D, KV), jnp.float32), pair)
        codes, scale = quantize(partial_sum)
        return (total + restore(codes, scale), None)
    grad, _ = lax.scan(node_step, jnp.zeros((D, KV), jnp.float32), (inputs, outputs))
    new_moment = 0.9 * moment + 0.1 * grad
    new_second = 0.95 * second + 0.05 * grad * grad
    first_fix = 1.0 - 0.9 ** 10
    second_fix = 1.0 - 0.95 ** 10
    update = new_moment / first_fix / (jnp.sqrt(new_second / second_fix) + 1e-08) + 0.1 * master
    new_master = master - 0.05 * update
    weight_copy = new_master.astype(jnp.bfloat16).reshape(N_NODE, D // N_NODE, KV)
    return (new_master, new_moment, new_second, weight_copy)
```

```python
import functools

import jax
import jax.numpy as jnp
from jax import lax
from jax.experimental import pallas as pl
from jax.experimental.pallas import tpu as pltpu
from jax.sharding import PartitionSpec as P

D = 8192
KV = 1024
TOK = 768
CHUNKS = 2
KVC = KV // CHUNKS
KB = KVC // 128
F32 = jnp.float32
BF16 = jnp.bfloat16
MIB = 1 << 20

MATCH = ((1, 0, 3, 2), (3, 2, 1, 0))


def bits(v):
    b = lax.shift_right_logical(v, 1)
    return (v ^ b) & 1, b


def local_perm(dim):
    m = MATCH[dim % 2]
    if dim < 2:
        return [(z * 4 + x, z * 4 + m[x]) for z in range(4) for x in range(4)]
    return [(z * 4 + x, m[z] * 4 + x) for z in range(4) for x in range(4)]


def y_perm(k):
    return [(n, ((n // 2 + k) % 4) * 2 + n % 2) for n in range(8)]


CORE_PERM = [(n, n ^ 1) for n in range(8)]


def pad16(n):
    return -(-n // 16) * 16


def code_rows(tiles):
    return tiles * KVC


def msg_rows(tiles):
    return tiles * KVC + pad16(tiles * KB)


def params(mib):
    return pltpu.CompilerParams(vmem_limit_bytes=mib * MIB)


def vmem():
    return pl.BlockSpec(memory_space=pltpu.VMEM)


def quantize(m):
    top = jnp.max(jnp.abs(m), axis=0, keepdims=True) + 1e-06
    scale = top.astype(BF16).astype(F32)
    return (m * (1.0 / scale)).astype(BF16), scale


def encode(m):
    top = jnp.max(jnp.abs(m), axis=0, keepdims=True) + 1e-30
    scale = top.astype(BF16).astype(F32)
    e = jnp.exp2(jnp.abs(m) * (250.0 / scale) - 125.0)
    return jnp.where(m < 0, -e, e).astype(BF16), scale


def decode(code, scale):
    y = code.astype(F32)
    m = (jnp.log2(jnp.abs(y)) + 125.0) * (scale * (1.0 / 250.0))
    return jnp.where(y < 0, -m, m)


def first_kernel(part, tok, og, send, keep, tokv, ogt, sc_send, sc_keep, sem):
    order = [(part + s) % 4 for s in range(4)]
    me_l = lax.axis_index("local")
    me_n = lax.axis_index("node")
    yp = (lax.shift_right_logical(me_n, 1) + part) & 3
    ax, bx = bits(me_l & 3)
    az, bz = bits(lax.shift_right_logical(me_l, 2))
    copies = []
    for q in range(4):
        b = (q >> 1) ^ bz
        z = 2 * b + ((q & 1) ^ az ^ b)
        for c in range(2):
            start = pl.multiple_of((yp * 2 + c) * 1024 + z * 256, 256)
            cp = pltpu.make_async_copy(tok.at[:, pl.ds(start, 256)], tokv.at[q, c], sem.at[q, c])
            cp.start()
            copies.append(cp)
    ogt[...] = og[...].T
    for q in range(4):
        copies[2 * q].wait()
        copies[2 * q + 1].wait()

    def pair(rel):
        xh = rel[1] ^ bx
        q = rel[2] + 2 * rel[3]
        lanes = pl.ds(pl.multiple_of(xh * 128, 128), 128)
        t0 = tokv[q, 0, :, lanes]
        t1 = tokv[q, 1, :, lanes]
        swap = (xh ^ ax) == 1
        even = jnp.concatenate([t0[:, :64], t1[:, :64]], axis=1)
        odd = jnp.concatenate([t0[:, 64:], t1[:, 64:]], axis=1)
        both = jnp.concatenate([jnp.where(swap, odd, even), jnp.where(swap, even, odd)], axis=1)
        g = jnp.dot(ogt[...], both, preferred_element_type=F32)
        for k in range(KB):
            code, scale = quantize(g[k * 128:(k + 1) * 128])
            for a in range(2):
                bit = {0: a, 1: rel[1], 2: rel[2], 3: rel[3]}
                out, sc = (send, sc_send) if bit[order[0]] is ONE or (order[0] == 0 and a == 1) else (keep, sc_keep)
                pos = bit[order[1]] * 4 + bit[order[2]] * 2 + bit[order[3]]
                row = pl.multiple_of(pos * KVC + k * 128, 128)
                out[pl.ds(row, 128), :] = code[:, a * 128:(a + 1) * 128]
                sc[pl.ds(pos * KB + k, 1), :] = scale[:, a * 128:(a + 1) * 128]

    if order[0] == 0:
        def body(t, _):
            pair({1: t & 1, 2: lax.shift_right_logical(t, 1) & 1, 3: lax.shift_right_logical(t, 2)})
            return 0
        lax.fori_loop(0, 8, body, 0)
    else:
        rest = [d for d in (1, 2, 3) if d != order[0]]

        def body(t, _):
            for v in (ONE, ZERO):
                pair({order[0]: v, rest[0]: t & 1, rest[1]: lax.shift_right_logical(t, 1)})
            return 0
        lax.fori_loop(0, 4, body, 0)
    send[code_rows(8):, :] = sc_send[...].astype(BF16)
    keep[code_rows(8):, :] = sc_keep[...].astype(BF16)


class Bit(int):
    pass


ZERO, ONE = Bit(0), Bit(1)


def first_stage(tokens, og, part):
    out = jax.ShapeDtypeStruct((msg_rows(8), 128), BF16)
    return pl.pallas_call(
        functools.partial(first_kernel, part),
        out_shape=(out, out),
        in_specs=[pl.BlockSpec(memory_space=pl.ANY), vmem()],
        out_specs=(vmem(), vmem()),
        scratch_shapes=[
            pltpu.VMEM((4, 2, TOK, 256), BF16),
            pltpu.VMEM((KVC, TOK), BF16),
            pltpu.VMEM((pad16(8 * KB), 128), F32),
            pltpu.VMEM((pad16(8 * KB), 128), F32),
            pltpu.SemaphoreType.DMA((4, 2)),
        ],
        compiler_params=params(24),
        cost_estimate=pl.CostEstimate(flops=2 * KVC * TOK * 2048, bytes_accessed=8 * MIB, transcendentals=0),
        name=f"grad_quantize_{part}",
    )(tokens, og)


def sum_kernel(tiles, coded, keep, recv, keep_out, send_out, sc_out):
    half = tiles // 2
    sc0 = code_rows(tiles)

    def total(block):
        rows = pl.ds(pl.multiple_of(block * 128, 128), 128)
        r_sc = recv[sc0:sc0 + pad16(tiles * KB), :].astype(F32)
        del r_sc
        return rows

    def body(block, _):
        rows = pl.ds(pl.multiple_of(block * 128, 128), 128)
        rs = sc_out[1, pl.ds(block, 1), :]
        if coded:
            m = keep[rows, :] + decode(recv[rows, :], rs)
        else:
            ks = sc_out[0, pl.ds(block, 1), :]
            m = keep[rows, :].astype(F32) * ks + recv[rows, :].astype(F32) * rs
        return m

    n = pad16(tiles * KB)
    sc_out[1, :n, :] = recv[sc0:sc0 + n, :].astype(F32)
    if not coded:
        sc_out[0, :n, :] = keep[sc0:sc0 + n, :].astype(F32)

    def keep_body(block, _):
        keep_out[pl.ds(pl.multiple_of(block * 128, 128), 128), :] = body(block, 0)
        return 0

    def send_body(block, _):
        code, scale = encode(body(block + half * KB, 0))
        send_out[pl.ds(pl.multiple_of(block * 128, 128), 128), :] = code
        sc_out[2, pl.ds(block, 1), :] = scale
        return 0

    lax.fori_loop(0, half * KB, send_body, 0, unroll=2)
    m = pad16(half * KB)
    send_out[code_rows(half):, :] = sc_out[2, :m, :].astype(BF16)
    lax.fori_loop(0, half * KB, keep_body, 0, unroll=2)


def sum_stage(keep, recv, tiles):
    half = tiles // 2
    n = pad16(tiles * KB)
    return pl.pallas_call(
        functools.partial(sum_kernel, tiles, tiles < 8),
        out_shape=(
            jax.ShapeDtypeStruct((code_rows(half), 128), F32),
            jax.ShapeDtypeStruct((msg_rows(half), 128), BF16),
        ),
        in_specs=[vmem(), vmem()],
        out_specs=(vmem(), vmem()),
        scratch_shapes=[pltpu.VMEM((3, n, 128), F32)],
        compiler_params=params(16),
        cost_estimate=pl.CostEstimate(flops=tiles * KVC * 128 * 10, bytes_accessed=tiles * KVC * 128 * 8, transcendentals=0),
        name=f"sum_{tiles}",
    )(keep, recv)


def requantize_kernel(keep, recv, out, sc):
    n = pad16(KB)
    sc[0] = recv[KVC:KVC + n, :].astype(F32)
    for k in range(KB):
        rows = slice(k * 128, (k + 1) * 128)
        m = keep[rows, :] + decode(recv[rows, :], sc[0, k:k + 1, :])
        code, scale = quantize(m)
        out[rows, :] = code
        sc[1, k:k + 1, :] = scale
    out[KVC:, :] = sc[1].astype(BF16)


def requantize_stage(keep, recv):
    return pl.pallas_call(
        requantize_kernel,
        out_shape=jax.ShapeDtypeStruct((msg_rows(1), 128), BF16),
        in_specs=[vmem(), vmem()],
        out_specs=vmem(),
        scratch_shapes=[pltpu.VMEM((2, pad16(KB), 128), F32)],
        compiler_params=params(8),
        cost_estimate=pl.CostEstimate(flops=KVC * 128 * 10, bytes_accessed=KVC * 128 * 8, transcendentals=0),
        name="requantize",
    )(keep, recv)


def node_sum_kernel(a, b, c, d, mine, other, sc, g):
    core = lax.axis_index("node") & 1
    n = pad16(KB)
    for i, r in enumerate((a, b, c, d)):
        sc[i] = r[KVC:KVC + n, :].astype(F32)
    for k in range(KB):
        rows = slice(k * 128, (k + 1) * 128)
        m = a[rows, :].astype(F32) * sc[0, k:k + 1, :]
        for i, r in ((1, b), (2, c), (3, d)):
            m = m + r[rows, :].astype(F32) * sc[i, k:k + 1, :]
        g[rows, :] = m
    h = KVC // 2
    lo = g[:h, :]
    hi = g[h:, :]
    first = jnp.concatenate([lo[:, :64], hi[:, :64]], axis=1)
    second = jnp.concatenate([lo[:, 64:], hi[:, 64:]], axis=1)
    mine[...] = jnp.where(core == 0, first, second)
    other[...] = jnp.where(core == 0, second, first)


def node_sum_stage(parts):
    out = jax.ShapeDtypeStruct((KVC // 2, 128), F32)
    return pl.pallas_call(
        node_sum_kernel,
        out_shape=(out, out),
        in_specs=[vmem()] * 4,
        out_specs=(vmem(), vmem()),
        scratch_shapes=[pltpu.VMEM((4, pad16(KB), 128), F32), pltpu.VMEM((KVC, 128), F32)],
        compiler_params=params(8),
        cost_estimate=pl.CostEstimate(flops=KVC * 128 * 10, bytes_accessed=KVC * 128 * 12, transcendentals=0),
        name="node_sum",
    )(*parts)


def adam_kernel(mine, recv, master, moment, second, new_master, new_moment, new_second, weight):
    t = (mine[...] + recv[...]).T
    grad = jnp.concatenate([t[:64], t[64:]], axis=1)
    m = 0.9 * moment[...] + 0.1 * grad
    s = 0.95 * second[...] + 0.05 * grad * grad
    update = m / (1.0 - 0.9**10) / (jnp.sqrt(s / (1.0 - 0.95**10)) + 1e-08) + 0.1 * master[...]
    w = master[...] - 0.05 * update
    new_master[...] = w
    new_moment[...] = m
    new_second[...] = s
    weight[...] = w.astype(BF16)


def adam_stage(mine, recv, master, moment, second, chunk):
    block = pl.BlockSpec((64, KVC), lambda i: (0, chunk))
    whole = pl.BlockSpec((KVC // 2, 128), lambda i: (0, 0))
    out = pl.BlockSpec((64, KVC), lambda i: (0, 0))
    f = jax.ShapeDtypeStruct((64, KVC), F32)
    return pl.pallas_call(
        adam_kernel,
        grid=(1,),
        out_shape=(f, f, f, jax.ShapeDtypeStruct((64, KVC), BF16)),
        in_specs=[whole, whole, block, block, block],
        out_specs=(out,) * 4,
        compiler_params=params(8),
        cost_estimate=pl.CostEstimate(flops=64 * KVC * 20, bytes_accessed=64 * KVC * 32, transcendentals=0),
        name="adam",
    )(mine, recv, master, moment, second)


def gather_kernel(*refs):
    me_n = lax.axis_index("node")
    y = lax.shift_right_logical(me_n, 1)
    core = me_n & 1
    pieces = refs[:CHUNKS * 11]
    new_master, new_moment, new_second, weight = refs[CHUNKS * 11:]
    for c in range(CHUNKS):
        p = pieces[c * 11:(c + 1) * 11]
        cols = slice(c * KVC, (c + 1) * KVC)
        new_master[:, cols] = p[0][...]
        new_moment[:, cols] = p[1][...]
        new_second[:, cols] = p[2][...]
        for k in range(4):
            src = ((y - k) & 3) * 2
            weight[src + core, :, cols] = p[3 + k][...]
            weight[src + 1 - core, :, cols] = p[7 + k][...]


def gather_stage(pieces):
    f = jax.ShapeDtypeStruct((64, KV), F32)
    return pl.pallas_call(
        gather_kernel,
        out_shape=(f, f, f, jax.ShapeDtypeStruct((8, 64, KV), BF16)),
        in_specs=[vmem()] * len(pieces),
        out_specs=(vmem(),) * 4,
        compiler_params=params(16),
        cost_estimate=pl.CostEstimate(flops=0, bytes_accessed=6 * MIB, transcendentals=0),
        name="gather_outputs",
    )(*pieces)


def local(tokens, out_grads, master, moment, second):
    og = [out_grads[:, c * KVC:(c + 1) * KVC] for c in range(CHUNKS)]
    units = [(c, p) for c in range(CHUNKS) for p in range(4)]
    keep, recv = {}, {}
    for u in units:
        c, p = u
        send, keep[u] = first_stage(tokens, og[c], p)
        recv[u] = lax.ppermute(send, "local", local_perm(p % 4))
    for s, tiles in ((1, 8), (2, 4), (3, 2)):
        for u in units:
            keep[u], send = sum_stage(keep[u], recv[u], tiles)
            recv[u] = lax.ppermute(send, "local", local_perm((u[1] + s) % 4))
    pieces = []
    for c in range(CHUNKS):
        parts = []
        for p in range(4):
            q = requantize_stage(keep[c, p], recv[c, p])
            parts.append(lax.ppermute(q, "node", y_perm(p)) if p else q)
        mine, other = node_sum_stage(parts)
        other = lax.ppermute(other, "node", CORE_PERM)
        a, b, d, w = adam_stage(mine, other, master, moment, second, c)
        own = [w] + [lax.ppermute(w, "node", y_perm(k)) for k in (1, 2, 3)]
        pieces += [a, b, d] + own + [lax.ppermute(v, "node", CORE_PERM) for v in own]
    return gather_stage(pieces)


def solution(mesh):
    rows = P(("node", "local"), None)
    return jax.shard_map(
        local,
        mesh=mesh,
        in_specs=(rows,) * 5,
        out_specs=(rows, rows, rows, P(None, "local", None)),
        check_vma=False,
    )
```

```python
import functools

import jax
import jax.numpy as jnp
from jax import lax
from jax.experimental import pallas as pl
from jax.experimental.pallas import tpu as pltpu
from jax.sharding import PartitionSpec as P

D = 8192
KV = 1024
TOK = 768
RUNS = KV // 128
HALF = KV // 2
PARTS = (2, 3, 0, 1)
F32 = jnp.float32
BF16 = jnp.bfloat16
MIB = 1 << 20
SMALL = pl.CostEstimate(flops=1, bytes_accessed=1, transcendentals=0)

MATCH = ((1, 0, 3, 2), (3, 2, 1, 0))


def bits(v):
    b = lax.shift_right_logical(v, 1)
    return (v ^ b) & 1, b


def local_perm(dim):
    m = MATCH[dim % 2]
    if dim < 2:
        return [(z * 4 + x, z * 4 + m[x]) for z in range(4) for x in range(4)]
    return [(z * 4 + x, m[z] * 4 + x) for z in range(4) for x in range(4)]


def y_perm(k):
    return [(n, ((n // 2 + k) % 4) * 2 + n % 2) for n in range(8)]


CORE_PERM = [(n, n ^ 1) for n in range(8)]


def pad16(n):
    return -(-n // 16) * 16


def code_rows(tiles):
    return tiles * KV


def msg_rows(tiles):
    return tiles * KV + pad16(tiles * RUNS)


def params(mib):
    return pltpu.CompilerParams(vmem_limit_bytes=mib * MIB)


def vmem():
    return pl.BlockSpec(memory_space=pltpu.VMEM)


def quantize(m):
    top = jnp.max(jnp.abs(m), axis=0, keepdims=True) + 1e-06
    scale = top.astype(BF16).astype(F32)
    return (m * (1.0 / scale)).astype(BF16), scale


def encode(m):
    top = jnp.max(jnp.abs(m), axis=0, keepdims=True) + 1e-30
    scale = top.astype(BF16).astype(F32)
    e = jnp.exp2(jnp.abs(m) * (250.0 / scale) - 125.0)
    return jnp.where(m < 0, -e, e).astype(BF16), scale


def decode(code, scale):
    y = code.astype(F32)
    m = (jnp.log2(jnp.abs(y)) + 125.0) * (scale * (1.0 / 250.0))
    return jnp.where(y < 0, -m, m)


def first_kernel(part, sent, load, first, tok, og_hbm, *refs):
    order = [(part + s) % 4 for s in range(4)]
    refs = list(refs)
    if not first:
        mine, ogt = refs.pop(0), refs.pop(0)
    refs.pop(0)
    out = refs.pop(0)
    if first:
        mine, ogt = refs.pop(0), refs.pop(0)
    if load is not None:
        ahead = refs.pop(0)
    sc, ogv, sem = refs
    me_l = lax.axis_index("local")
    me_n = lax.axis_index("node")
    y = lax.shift_right_logical(me_n, 1)
    ax, bx = bits(me_l & 3)
    az, bz = bits(lax.shift_right_logical(me_l, 2))

    def fetch(p, to, z, c, s):
        source = pl.multiple_of(((y + p) & 3) * 2048 + c * 1024 + z * 256, 256)
        to_lane = pl.multiple_of(c * 1024 + z * 256, 256)
        return pltpu.make_async_copy(tok.at[:, pl.ds(source, 256)], to.at[:, pl.ds(to_lane, 256)], sem.at[s])

    def place_z(a, b):
        zb = b ^ bz
        return 2 * zb + (a ^ az ^ zb)

    def pairs(t):
        lo, hi = t & 1, t >> 1 if isinstance(t, int) else lax.shift_right_logical(t, 1)
        return {0: [(0, lo, hi), (1, lo, hi)], 1: [(sent, lo, hi)], 2: [(lo, sent, hi)], 3: [(lo, hi, sent)]}[order[0]]

    wait, rest = {}, []
    if first:
        ogc = pltpu.make_async_copy(og_hbm, ogv, sem.at[16])
        ogc.start()
        used = []
        for t in range(4):
            for _, a, b in pairs(t):
                if (a, b) not in used:
                    used.append((a, b))
        late = [(a, b) for a in range(2) for b in range(2) if (a, b) not in used]
        for i, (a, b) in enumerate(used + late):
            cs = [fetch(part, mine, place_z(a, b), c, 2 * i + c) for c in range(2)]
            for cp in cs:
                cp.start()
            if i < len(used):
                wait[a, b] = cs
            else:
                rest += cs
    if load is not None:
        for z in range(4):
            for c in range(2):
                rest.append(fetch(load, ahead, z, c, 8 + 2 * z + c))
                rest[-1].start()
    if first:
        ogc.wait()
        ogt[...] = ogv[...].T

    def body(t, _):
        columns, places = [], []
        for x, a, b in pairs(t):
            for cp in wait.pop((a, b), ()) if first else ():
                cp.wait()
            lane = place_z(a, b) * 256 + (x ^ bx) * 128
            t0 = mine[:, pl.ds(pl.multiple_of(lane, 128), 128)]
            t1 = mine[:, pl.ds(pl.multiple_of(lane + 1024, 128), 128)]
            swap = (x ^ bx ^ ax) == 1
            even = jnp.concatenate([t0[:, :64], t1[:, :64]], axis=1)
            odd = jnp.concatenate([t0[:, 64:], t1[:, 64:]], axis=1)
            for d in (sent,) if order[0] == 0 else (0, 1):
                columns.append(jnp.where(swap, even, odd) if d else jnp.where(swap, odd, even))
                bit = (d, x, a, b)
                places.append(bit[order[1]] * 4 + bit[order[2]] * 2 + bit[order[3]])
        both = jnp.concatenate(columns, axis=1)
        grad = jnp.dot(ogt[...], both, preferred_element_type=F32)
        for k in range(RUNS):
            code, scale = quantize(grad[k * 128:(k + 1) * 128])
            for i, place in enumerate(places):
                row = place * KV + k * 128
                row = row if isinstance(row, int) else pl.multiple_of(row, 128)
                out[pl.ds(row, 128), :] = code[:, i * 128:(i + 1) * 128]
                sc[pl.ds(place * RUNS + k, 1), :] = scale[:, i * 128:(i + 1) * 128]
        return 0

    if first:
        for t in range(4):
            body(t, 0)
    else:
        lax.fori_loop(0, 4, body, 0)
    out[code_rows(8):, :] = sc[...].astype(BF16)
    for cp in rest:
        cp.wait()


def first_stage(tokens, out_grads, part, sent, load, mine, ogt, after):
    first = mine is None
    held = jax.ShapeDtypeStruct((TOK, 2048), BF16)
    made = jax.ShapeDtypeStruct((KV, TOK), BF16)
    out = [jax.ShapeDtypeStruct((msg_rows(8), 128), BF16)] + [held, made] * first + [held] * (load is not None)
    args = [] if first else [mine, ogt]
    anywhere = pl.BlockSpec(memory_space=pl.ANY)
    return pl.pallas_call(
        functools.partial(first_kernel, part, sent, load, first),
        out_shape=tuple(out),
        in_specs=[anywhere, anywhere] + [vmem()] * len(args) + [anywhere],
        out_specs=tuple(vmem() for _ in out),
        scratch_shapes=[
            pltpu.VMEM((pad16(8 * RUNS), 128), F32),
            pltpu.VMEM((TOK, KV) if first else (16, 128), BF16),
            pltpu.SemaphoreType.DMA((17,)),
        ],
        compiler_params=params(18),
        cost_estimate=SMALL,
        name=f"grad_{'send' if sent else 'keep'}_{part}",
    )(tokens, out_grads, *args, after)


def sum_kernel(tiles, kb, coded, n, *refs):
    half = tiles // 2
    keeps, recvs = refs[:n], refs[n:2 * n]
    keep_out, send_out, sc_keep, sc_recv, sc_send = refs[2 * n + 1:]
    rows = tiles * kb
    for j in range(n):
        sc_recv[j] = recvs[j][rows * 128:, :].astype(F32)
        if not coded:
            sc_keep[j] = keeps[j][rows * 128:, :].astype(F32)

    def total(j, block):
        r = pl.ds(pl.multiple_of(block * 128, 128), 128)
        scale = sc_recv[j, pl.ds(block, 1), :]
        if coded:
            return keeps[j][r, :] + decode(recvs[j][r, :], scale)
        return keeps[j][r, :].astype(F32) * sc_keep[j, pl.ds(block, 1), :] + recvs[j][r, :].astype(F32) * scale

    def place(j, block):
        if n == 1:
            return block
        return lax.div(block, kb) * (n * kb) + j * kb + lax.rem(block, kb)

    for j in range(n):
        def send_body(block, _):
            code, scale = encode(total(j, block + half * kb))
            to = place(j, block)
            send_out[pl.ds(pl.multiple_of(to * 128, 128), 128), :] = code
            sc_send[pl.ds(to, 1), :] = scale
            return 0

        lax.fori_loop(0, half * kb, send_body, 0, unroll=2)
    send_out[n * half * kb * 128:, :] = sc_send[...].astype(BF16)
    for j in range(n):
        def keep_body(block, _):
            keep_out[pl.ds(pl.multiple_of(place(j, block) * 128, 128), 128), :] = total(j, block)
            return 0

        lax.fori_loop(0, half * kb, keep_body, 0, unroll=2)


def sum_stage(keeps, recvs, tiles, kb, after):
    n = len(keeps)
    half = n * tiles // 2 * kb
    return pl.pallas_call(
        functools.partial(sum_kernel, tiles, kb, tiles < 8, n),
        out_shape=(
            jax.ShapeDtypeStruct((half * 128, 128), F32),
            jax.ShapeDtypeStruct((half * 128 + pad16(half), 128), BF16),
        ),
        in_specs=[vmem()] * (2 * n) + [pl.BlockSpec(memory_space=pl.ANY)],
        out_specs=(vmem(), vmem()),
        scratch_shapes=[
            pltpu.VMEM((n, pad16(tiles * kb), 128), F32),
            pltpu.VMEM((n, pad16(tiles * kb), 128), F32),
            pltpu.VMEM((pad16(half), 128), F32),
        ],
        compiler_params=params(16),
        cost_estimate=SMALL,
        name=f"sum_{tiles}",
    )(*keeps, *recvs, after)


def pack(lo, hi, core):
    first = jnp.concatenate([lo[:, :64], hi[:, :64]], axis=1)
    second = jnp.concatenate([lo[:, 64:], hi[:, 64:]], axis=1)
    return jnp.where(core == 0, first, second), jnp.where(core == 0, second, first)


def requantize_kernel(keep, recv, _, mine, other, sc):
    core = lax.axis_index("node") & 1
    sc[0] = recv[KV:KV + 16, :].astype(F32)
    for k in range(RUNS // 2):
        made = []
        for j in (k, k + RUNS // 2):
            rows = slice(j * 128, (j + 1) * 128)
            made.append(quantize(keep[rows, :] + decode(recv[rows, :], sc[0, j:j + 1, :])))
        codes = pack(made[0][0], made[1][0], core)
        scales = pack(made[0][1], made[1][1], core)
        for i, out in enumerate((mine, other)):
            out[k * 128:(k + 1) * 128, :] = codes[i]
            sc[1 + i, k:k + 1, :] = scales[i]
    mine[HALF:, :] = sc[1].astype(BF16)
    other[HALF:, :] = sc[2].astype(BF16)


def requantize_stage(keep, recv, after):
    out = jax.ShapeDtypeStruct((HALF + 16, 128), BF16)
    return pl.pallas_call(
        requantize_kernel,
        out_shape=(out, out),
        in_specs=[vmem(), vmem(), pl.BlockSpec(memory_space=pl.ANY)],
        out_specs=(vmem(), vmem()),
        scratch_shapes=[pltpu.VMEM((3, 16, 128), F32)],
        compiler_params=params(8),
        cost_estimate=SMALL,
        name="requantize",
    )(keep, recv, after)


def core_sum_kernel(coded, mine, recv, _, out, sc):
    sc[0] = mine[HALF:, :].astype(F32)
    sc[1] = recv[HALF:, :].astype(F32)
    for k in range(RUNS // 2):
        rows = slice(k * 128, (k + 1) * 128)
        m = mine[rows, :].astype(F32) * sc[0, k:k + 1, :] + recv[rows, :].astype(F32) * sc[1, k:k + 1, :]
        if coded:
            m, sc[2, k:k + 1, :] = encode(m)
        out[rows, :] = m
    if coded:
        out[HALF:, :] = sc[2].astype(BF16)


def core_sum_stage(mine, recv, coded, after):
    out = jax.ShapeDtypeStruct((HALF + 16, 128), BF16) if coded else jax.ShapeDtypeStruct((HALF, 128), F32)
    return pl.pallas_call(
        functools.partial(core_sum_kernel, coded),
        out_shape=out,
        in_specs=[vmem(), vmem(), pl.BlockSpec(memory_space=pl.ANY)],
        out_specs=vmem(),
        scratch_shapes=[pltpu.VMEM((3, 16, 128), F32)],
        compiler_params=params(8),
        cost_estimate=SMALL,
        name="core_sum",
    )(mine, recv, after)


def adam_rule(grad, master, moment, second):
    m = 0.9 * moment + 0.1 * grad
    s = 0.95 * second + 0.05 * grad * grad
    update = m / (1.0 - 0.9**10) / (jnp.sqrt(s / (1.0 - 0.95**10)) + 1e-08) + 0.1 * master
    return master - 0.05 * update, m, s


def weight_kernel(own, a, b, c, master, moment, second, weight, grad, sc, g):
    for i, r in enumerate((a, b, c)):
        sc[i] = r[HALF:, :].astype(F32)
    for k in range(RUNS // 2):
        rows = slice(k * 128, (k + 1) * 128)
        m = own[rows, :]
        for i, r in enumerate((a, b, c)):
            m = m + decode(r[rows, :], sc[i, k:k + 1, :])
        g[rows, :] = m
    t = g[...].T
    whole = jnp.concatenate([t[:64], t[64:]], axis=1)
    grad[...] = whole
    weight[...] = adam_rule(whole, master[...], moment[...], second[...])[0].astype(BF16)


def weight_stage(own, others, master, moment, second):
    return pl.pallas_call(
        weight_kernel,
        out_shape=(jax.ShapeDtypeStruct((64, KV), BF16), jax.ShapeDtypeStruct((64, KV), F32)),
        in_specs=[vmem()] * 7,
        out_specs=(vmem(),) * 2,
        scratch_shapes=[pltpu.VMEM((3, 16, 128), F32), pltpu.VMEM((HALF, 128), F32)],
        compiler_params=params(8),
        cost_estimate=SMALL,
        name="adam_weight",
    )(own, *others, master, moment, second)


def adam_kernel(grad, master, moment, second, _, new_master, new_moment, new_second):
    new_master[...], new_moment[...], new_second[...] = adam_rule(grad[...], master[...], moment[...], second[...])


def adam_stage(grad, master, moment, second, after):
    f = jax.ShapeDtypeStruct((64, KV), F32)
    return pl.pallas_call(
        adam_kernel,
        out_shape=(f, f, f),
        in_specs=[vmem()] * 4 + [pl.BlockSpec(memory_space=pl.ANY)],
        out_specs=(vmem(),) * 3,
        compiler_params=params(8),
        cost_estimate=pl.CostEstimate(flops=64 * KV * 20, bytes_accessed=64 * KV * 32, transcendentals=0),
        name="adam",
    )(grad, master, moment, second, after)


def gather_kernel(*refs):
    me_n = lax.axis_index("node")
    y = lax.shift_right_logical(me_n, 1)
    core = me_n & 1
    weight = refs[8]
    for k in range(4):
        src = ((y - k) & 3) * 2
        weight[src + core] = refs[k][...]
        weight[src + 1 - core] = refs[4 + k][...]


def gather_stage(pieces):
    return pl.pallas_call(
        gather_kernel,
        out_shape=jax.ShapeDtypeStruct((8, 64, KV), BF16),
        in_specs=[vmem()] * 8,
        out_specs=vmem(),
        compiler_params=params(16),
        cost_estimate=SMALL,
        name="gather_weights",
    )(*pieces)


def local(tokens, out_grads, master, moment, second):
    tokens = pltpu.with_memory_space_constraint(tokens, pltpu.HBM)
    out_grads = pltpu.with_memory_space_constraint(out_grads, pltpu.HBM)
    keep, recv, held = {}, {}, {}
    after, ogt = out_grads, None
    for i, p in enumerate(PARTS):
        load = PARTS[i + 1] if i < 3 else None
        send, *more = first_stage(tokens, out_grads, p, 1, load, held.get(p), ogt, after)
        if i == 0:
            held[p], ogt = more.pop(0), more.pop(0)
        if load is not None:
            held[load], = more
        after = send
        recv[p] = lax.ppermute(send, "local", local_perm(p))
    for p in PARTS:
        keep[p], = first_stage(tokens, out_grads, p, 0, None, held[p], ogt, after)
        after = keep[p]
    for step, tiles in ((1, 8), (2, 4), (3, 2)):
        for p in PARTS:
            keep[p], send = sum_stage([keep[p]], [recv[p]], tiles, RUNS, after)
            after = send
            recv[p] = lax.ppermute(send, "local", local_perm((p + step) % 4))
    mine, other = {}, {}
    for p in PARTS:
        mine[p], other[p] = requantize_stage(keep[p], recv[p], after)
        after = mine[p]
        other[p] = lax.ppermute(other[p], "node", CORE_PERM)
    parts = {}
    for p in PARTS:
        after = core_sum_stage(mine[p], other[p], p > 0, after)
        parts[p] = lax.ppermute(after, "node", y_perm(p)) if p else after
    w, grad = weight_stage(parts[0], [parts[p] for p in (1, 2, 3)], master, moment, second)
    own = [w] + [lax.ppermute(w, "node", y_perm(k)) for k in (1, 2, 3)]
    a, b, d = adam_stage(grad, master, moment, second, w)
    weight = gather_stage(own + [lax.ppermute(v, "node", CORE_PERM) for v in own])
    return a, b, d, weight


def solution(mesh):
    rows = P(("node", "local"), None)
    return jax.shard_map(
        local,
        mesh=mesh,
        in_specs=(rows,) * 5,
        out_specs=(rows, rows, rows, P(None, "local", None)),
        check_vma=False,
    )
```

```python
import functools

import jax
import jax.numpy as jnp
from jax import lax
from jax.experimental import pallas as pl
from jax.experimental.pallas import tpu as pltpu
from jax.sharding import PartitionSpec as P

D = 8192
KV = 1024
TOK = 768
RUNS = KV // 128
HALF = KV // 2
PARTS = (1, 2, 3, 0)
EARLY = 2
SENT_AT = {1: 0, 2: 1024, 3: 2048, 0: 3072}
KEPT_AT = {1: 0, 2: 1024, 3: 2048}
HELD = (3072, 5120)
F32 = jnp.float32
BF16 = jnp.bfloat16
MIB = 1 << 20
SMALL = pl.CostEstimate(flops=1, bytes_accessed=1, transcendentals=0)

MATCH = ((1, 0, 3, 2), (3, 2, 1, 0))


def bits(v):
    b = lax.shift_right_logical(v, 1)
    return (v ^ b) & 1, b


def local_perm(dim):
    m = MATCH[dim % 2]
    if dim < 2:
        return [(z * 4 + x, z * 4 + m[x]) for z in range(4) for x in range(4)]
    return [(z * 4 + x, m[z] * 4 + x) for z in range(4) for x in range(4)]


def y_perm(k):
    return [(n, ((n // 2 + k) % 4) * 2 + n % 2) for n in range(8)]


CORE_PERM = [(n, n ^ 1) for n in range(8)]


def pad16(n):
    return -(-n // 16) * 16


def msg_rows(blocks):
    return blocks * 128 + pad16(blocks)


def params(mib):
    return pltpu.CompilerParams(vmem_limit_bytes=mib * MIB)


def vmem():
    return pl.BlockSpec(memory_space=pltpu.VMEM)


def quantize(m):
    top = jnp.max(jnp.abs(m), axis=0, keepdims=True) + 1e-06
    scale = top.astype(BF16).astype(F32)
    return (m * (1.0 / scale)).astype(BF16), scale


def encode(m):
    top = jnp.max(jnp.abs(m), axis=0, keepdims=True) + 1e-30
    scale = top.astype(BF16).astype(F32)
    e = jnp.exp2(jnp.abs(m) * (250.0 / scale) - 125.0)
    return jnp.where(m < 0, -e, e).astype(BF16), scale


def decode(code, scale):
    y = code.astype(F32)
    m = (jnp.log2(jnp.abs(y)) + 125.0) * (scale * (1.0 / 250.0))
    return jnp.where(y < 0, -m, m)


GROUPS = {"early": (0, EARLY), "late": (EARLY, RUNS)}


def aligned(v):
    return v if isinstance(v, int) else pl.multiple_of(v, 128)


def first_kernel(part, sent, group, fetch, *refs):
    order = [(part + s) % 4 for s in range(4)]
    if fetch and sent:
        tok, og, _, out, held, ogt, sc, sem, ogv = refs
    elif fetch:
        tok, ogt, _, out, held, sc, sem = refs
    else:
        held, ogt, _, out, sc = refs
    k0, k1 = GROUPS.get(group, (0, RUNS))
    me_l = lax.axis_index("local")
    ax, bx = bits(me_l & 3)
    az, bz = bits(lax.shift_right_logical(me_l, 2))

    def place_z(a, b):
        zb = b ^ bz
        return 2 * zb + (a ^ az ^ zb)

    if fetch:
        y = lax.shift_right_logical(lax.axis_index("node"), 1)
        copies = []
        if sent:
            copies.append(pltpu.make_async_copy(og, ogv, sem.at[0]))
        for p, at in (SENT_AT if sent else KEPT_AT).items():
            base = ((y + p) & 3) * 2048
            if p == 0:
                for i in range(4):
                    rows = pl.ds(i * TOK // 4, TOK // 4)
                    copies.append(pltpu.make_async_copy(
                        tok.at[rows, pl.ds(pl.multiple_of(base, 2048), 2048)],
                        held.at[rows, at:at + 2048],
                        sem.at[len(copies)],
                    ))
                continue
            for u in range(4 if p == 1 else 2):
                width = 128 if p == 1 else 256
                a, b = {1: (u & 1, u >> 1), 2: (sent, u), 3: (u, sent)}[p]
                lane = place_z(a, b) * 256 + ((sent ^ bx) * 128 if p == 1 else 0)
                for c in range(2):
                    to = at + c * 512 + u * width
                    copies.append(pltpu.make_async_copy(
                        tok.at[:, pl.ds(aligned(base + c * 1024 + lane), width)],
                        held.at[:, to:to + width],
                        sem.at[len(copies)],
                    ))
        for cp in copies:
            cp.start()
        if sent:
            copies.pop(0).wait()
            ogt[...] = ogv[...].T
        for cp in copies[:8]:
            cp.wait()

    for t in range(4):
        columns, places = [], []
        lo, hi = t & 1, t >> 1
        for x, a, b in {
            0: [(0, lo, hi), (1, lo, hi)], 1: [(sent, lo, hi)], 2: [(lo, sent, hi)], 3: [(lo, hi, sent)]
        }[part]:
            half = 512 if part else 1024
            lane = (SENT_AT if sent or not part else KEPT_AT)[part] + {
                0: place_z(a, b) * 256 + (x ^ bx) * 128,
                1: (a + 2 * b) * 128,
                2: b * 256 + (x ^ bx) * 128,
                3: a * 256 + (x ^ bx) * 128,
            }[part]
            t0 = held[:, pl.ds(aligned(lane), 128)]
            t1 = held[:, pl.ds(aligned(lane + half), 128)]
            swap = (x ^ bx ^ ax) == 1
            even = jnp.concatenate([t0[:, :64], t1[:, :64]], axis=1)
            odd = jnp.concatenate([t0[:, 64:], t1[:, 64:]], axis=1)
            for d in (sent,) if part == 0 else (0, 1):
                columns.append(jnp.where(swap, even, odd) if d else jnp.where(swap, odd, even))
                bit = (d, x, a, b)
                places.append(bit[order[1]] * 4 + bit[order[2]] * 2 + bit[order[3]])
        grad = jnp.dot(ogt[k0 * 128:k1 * 128, :], jnp.concatenate(columns, axis=1), preferred_element_type=F32)
        for k in range(k1 - k0):
            code, scale = quantize(grad[k * 128:(k + 1) * 128])
            for i, place in enumerate(places):
                block = place * (k1 - k0) + k
                out[block * 128:(block + 1) * 128, :] = code[:, i * 128:(i + 1) * 128]
                sc[block:block + 1, :] = scale[:, i * 128:(i + 1) * 128]
    out[8 * (k1 - k0) * 128:, :] = sc[...].astype(BF16)
    if fetch:
        for cp in copies[8:]:
            cp.wait()


def first_stage(part, sent, group, args, after, fetch=False):
    k0, k1 = GROUPS.get(group, (0, RUNS))
    blocks = 8 * (k1 - k0)
    out = [jax.ShapeDtypeStruct((msg_rows(blocks), 128), BF16)]
    scratch = [pltpu.VMEM((blocks, 128), F32)]
    anywhere = pl.BlockSpec(memory_space=pl.ANY)
    specs = [vmem()] * 2
    if fetch:
        out.append(jax.ShapeDtypeStruct((TOK, HELD[sent]), BF16))
        scratch.append(pltpu.SemaphoreType.DMA((21,)))
        specs = [anywhere] * 2 if sent else [anywhere, vmem()]
        if sent:
            out.append(jax.ShapeDtypeStruct((KV, TOK), BF16))
            scratch.append(pltpu.VMEM((TOK, KV), BF16))
    return pl.pallas_call(
        functools.partial(first_kernel, part, sent, group, fetch),
        out_shape=tuple(out),
        in_specs=specs + [anywhere],
        out_specs=tuple(vmem() for _ in out),
        scratch_shapes=scratch,
        compiler_params=params(20),
        cost_estimate=SMALL,
        name=f"grad_{'send' if sent else 'keep'}_{part}",
    )(*args, after)


def hold(message, after):
    anywhere = pl.BlockSpec(memory_space=pl.ANY)
    return pl.pallas_call(
        lambda message, _, out: None,
        out_shape=jax.ShapeDtypeStruct(message.shape, message.dtype),
        in_specs=[anywhere, anywhere],
        out_specs=anywhere,
        input_output_aliases={0: 0},
        compiler_params=params(1),
        cost_estimate=SMALL,
        name="hold",
    )(message, after)


def sum_kernel(tiles, send, n, *refs):
    half = tiles // 2
    keep, recvs = refs[0], refs[1:1 + n]
    out, sc_keep, sc_recv, sc_out = refs[2 + n:]
    coded = tiles < 8
    counts = [EARLY, RUNS - EARLY] if n == 2 else [RUNS]
    for j, r in enumerate(recvs):
        rows = pad16(tiles * counts[j])
        sc_recv[j, :rows, :] = r[tiles * counts[j] * 128:, :].astype(F32)
    if not coded:
        sc_keep[...] = keep[tiles * RUNS * 128:, :].astype(F32)

    def body(t, _):
        source = t + half if send else t
        k = 0
        for j, r in enumerate(recvs):
            for i in range(counts[j]):
                block = source * RUNS + k
                kept = keep[pl.ds(aligned(block * 128), 128), :]
                there = source * counts[j] + i
                came = r[pl.ds(aligned(there * 128), 128), :]
                scale = sc_recv[j, pl.ds(there, 1), :]
                if coded:
                    m = kept + decode(came, scale)
                else:
                    m = kept.astype(F32) * sc_keep[pl.ds(block, 1), :] + came.astype(F32) * scale
                to = t * RUNS + k
                if send:
                    m, scale = encode(m)
                    sc_out[pl.ds(to, 1), :] = scale
                out[pl.ds(aligned(to * 128), 128), :] = m
                k += 1
        return 0

    if half == 1:
        body(0, 0)
    else:
        lax.fori_loop(0, half, body, 0)
    if send:
        out[half * RUNS * 128:, :] = sc_out[...].astype(BF16)


def sum_stage(keep, recvs, tiles, send, after):
    n = len(recvs)
    half = tiles // 2 * RUNS
    return pl.pallas_call(
        functools.partial(sum_kernel, tiles, send, n),
        out_shape=jax.ShapeDtypeStruct((msg_rows(half), 128), BF16) if send else jax.ShapeDtypeStruct((half * 128, 128), F32),
        in_specs=[vmem()] * (1 + n) + [pl.BlockSpec(memory_space=pl.ANY)],
        out_specs=vmem(),
        scratch_shapes=[
            pltpu.VMEM((pad16(tiles * RUNS), 128), F32),
            pltpu.VMEM((n, pad16(tiles * RUNS), 128), F32),
            pltpu.VMEM((pad16(half), 128), F32),
        ],
        compiler_params=params(16),
        cost_estimate=SMALL,
        name=f"sum_{'send' if send else 'keep'}_{tiles}",
    )(keep, *recvs, after)


def pack(lo, hi, core):
    first = jnp.concatenate([lo[:, :64], hi[:, :64]], axis=1)
    second = jnp.concatenate([lo[:, 64:], hi[:, 64:]], axis=1)
    return jnp.where(core == 0, first, second), jnp.where(core == 0, second, first)


def requantize_kernel(keep, recv, _, mine, other, sc):
    core = lax.axis_index("node") & 1
    sc[0] = recv[KV:KV + 16, :].astype(F32)
    for k in range(RUNS // 2):
        made = []
        for j in (k, k + RUNS // 2):
            rows = slice(j * 128, (j + 1) * 128)
            made.append(quantize(keep[rows, :] + decode(recv[rows, :], sc[0, j:j + 1, :])))
        codes = pack(made[0][0], made[1][0], core)
        scales = pack(made[0][1], made[1][1], core)
        for i, out in enumerate((mine, other)):
            out[k * 128:(k + 1) * 128, :] = codes[i]
            sc[1 + i, k:k + 1, :] = scales[i]
    mine[HALF:, :] = sc[1].astype(BF16)
    other[HALF:, :] = sc[2].astype(BF16)


def requantize_stage(keep, recv, after):
    out = jax.ShapeDtypeStruct((HALF + 16, 128), BF16)
    return pl.pallas_call(
        requantize_kernel,
        out_shape=(out, out),
        in_specs=[vmem(), vmem(), pl.BlockSpec(memory_space=pl.ANY)],
        out_specs=(vmem(), vmem()),
        scratch_shapes=[pltpu.VMEM((3, 16, 128), F32)],
        compiler_params=params(8),
        cost_estimate=SMALL,
        name="requantize",
    )(keep, recv, after)


def core_sum_kernel(coded, mine, recv, _, out, sc):
    sc[0] = mine[HALF:, :].astype(F32)
    sc[1] = recv[HALF:, :].astype(F32)
    for k in range(RUNS // 2):
        rows = slice(k * 128, (k + 1) * 128)
        m = mine[rows, :].astype(F32) * sc[0, k:k + 1, :] + recv[rows, :].astype(F32) * sc[1, k:k + 1, :]
        if coded:
            m, sc[2, k:k + 1, :] = encode(m)
        out[rows, :] = m
    if coded:
        out[HALF:, :] = sc[2].astype(BF16)


def core_sum_stage(mine, recv, coded, after):
    out = jax.ShapeDtypeStruct((HALF + 16, 128), BF16) if coded else jax.ShapeDtypeStruct((HALF, 128), F32)
    return pl.pallas_call(
        functools.partial(core_sum_kernel, coded),
        out_shape=out,
        in_specs=[vmem(), vmem(), pl.BlockSpec(memory_space=pl.ANY)],
        out_specs=vmem(),
        scratch_shapes=[pltpu.VMEM((3, 16, 128), F32)],
        compiler_params=params(8),
        cost_estimate=SMALL,
        name="core_sum",
    )(mine, recv, after)


def adam_rule(grad, master, moment, second):
    m = 0.9 * moment + 0.1 * grad
    s = 0.95 * second + 0.05 * grad * grad
    update = m / (1.0 - 0.9**10) / (jnp.sqrt(s / (1.0 - 0.95**10)) + 1e-08) + 0.1 * master
    return master - 0.05 * update, m, s


def weight_kernel(own, a, b, c, master, moment, second, weight, grad, sc, g):
    for i, r in enumerate((a, b, c)):
        sc[i] = r[HALF:, :].astype(F32)
    for k in range(RUNS // 2):
        rows = slice(k * 128, (k + 1) * 128)
        m = own[rows, :]
        for i, r in enumerate((a, b, c)):
            m = m + decode(r[rows, :], sc[i, k:k + 1, :])
        g[rows, :] = m
    t = g[...].T
    whole = jnp.concatenate([t[:64], t[64:]], axis=1)
    grad[...] = whole
    weight[...] = adam_rule(whole, master[...], moment[...], second[...])[0].astype(BF16)


def weight_stage(own, others, master, moment, second):
    return pl.pallas_call(
        weight_kernel,
        out_shape=(jax.ShapeDtypeStruct((64, KV), BF16), jax.ShapeDtypeStruct((64, KV), F32)),
        in_specs=[vmem()] * 7,
        out_specs=(vmem(),) * 2,
        scratch_shapes=[pltpu.VMEM((3, 16, 128), F32), pltpu.VMEM((HALF, 128), F32)],
        compiler_params=params(8),
        cost_estimate=SMALL,
        name="adam_weight",
    )(own, *others, master, moment, second)


def adam_kernel(grad, master, moment, second, new_master, new_moment, new_second, mark):
    mark[...] = jnp.zeros_like(mark)
    new_master[...], new_moment[...], new_second[...] = adam_rule(grad[...], master[...], moment[...], second[...])


def adam_stage(*arrays):
    f = jax.ShapeDtypeStruct((64, KV), F32)
    return pl.pallas_call(
        adam_kernel,
        out_shape=(f, f, f, jax.ShapeDtypeStruct((8, 128), F32)),
        in_specs=[vmem()] * 4,
        out_specs=(vmem(),) * 4,
        compiler_params=params(8),
        cost_estimate=SMALL,
        name="adam",
    )(*arrays)


def gather_kernel(*refs):
    me_n = lax.axis_index("node")
    y = lax.shift_right_logical(me_n, 1)
    core = me_n & 1
    weight = refs[8]
    for k in range(4):
        src = ((y - k) & 3) * 2
        weight[src + core] = refs[k][...]
        weight[src + 1 - core] = refs[4 + k][...]


def gather_stage(weights):
    return pl.pallas_call(
        gather_kernel,
        out_shape=jax.ShapeDtypeStruct((8, 64, KV), BF16),
        in_specs=[vmem()] * 8,
        out_specs=vmem(),
        compiler_params=params(8),
        cost_estimate=SMALL,
        name="gather",
    )(*weights)


def local(tokens, out_grads, master, moment, second):
    tokens = pltpu.with_memory_space_constraint(tokens, pltpu.HBM)
    out_grads = pltpu.with_memory_space_constraint(out_grads, pltpu.HBM)
    keep, recv, early, late = {}, {}, {}, {}
    after, args = out_grads, (tokens, out_grads)
    for i, p in enumerate(PARTS):
        after, *more = first_stage(p, 1, "early", args, after, i == 0)
        args = tuple(more) or args
        early[p] = lax.ppermute(after, "local", local_perm(p))
    for p in PARTS:
        after, = first_stage(p, 1, "late", args, after)
        late[p] = after
    for p in PARTS:
        after = hold(late[p], early[p])
        recv[p] = [early[p], lax.ppermute(after, "local", local_perm(p))]
    held, ogt = args
    for i, p in enumerate(PARTS):
        after, *more = first_stage(p, 0, None, (tokens if i == 0 else args[0] if p == 0 else held, ogt), after, i == 0)
        held, = more or [held]
        keep[p] = after
    for step, tiles in ((1, 8), (2, 4), (3, 2)):
        arrived = dict(recv)
        for p in PARTS:
            after = sum_stage(keep[p], arrived[p], tiles, True, after)
            recv[p] = [lax.ppermute(after, "local", local_perm((p + step) % 4))]
        for p in PARTS:
            after = keep[p] = sum_stage(keep[p], arrived[p], tiles, False, after)
    mine, other, parts = {}, {}, {}
    one, two, three, own = PARTS
    for p, summed in ((one, None), (two, one), (three, two), (own, three), (None, own)):
        if p is not None:
            mine[p], other[p] = requantize_stage(keep[p], recv[p][0], after)
            after = mine[p]
            other[p] = lax.ppermute(other[p], "node", CORE_PERM)
        if summed is not None:
            after = core_sum_stage(mine[summed], other[summed], summed > 0, after)
            parts[summed] = lax.ppermute(after, "node", y_perm(summed)) if summed else after
    w, grad = weight_stage(parts[0], [parts[p] for p in (1, 2, 3)], master, moment, second)
    own = [w] + [lax.ppermute(w, "node", y_perm(k)) for k in (1, 2, 3)]
    *new, mark = adam_stage(grad, master, moment, second)
    own[3] = hold(own[3], mark)
    own += [lax.ppermute(v, "node", CORE_PERM) for v in own]
    return (*new, gather_stage(own))


def solution(mesh):
    rows = P(("node", "local"), None)
    return jax.shard_map(
        local,
        mesh=mesh,
        in_specs=(rows,) * 5,
        out_specs=(rows, rows, rows, P(None, "local", None)),
        check_vma=False,
    )
```

```python
import functools

import jax
import jax.numpy as jnp
from jax import lax
from jax.experimental import pallas as pl
from jax.experimental.pallas import tpu as pltpu
from jax.sharding import PartitionSpec as P

D = 8192
KV = 1024
TOK = 768
RUNS = KV // 128
HALF = KV // 2
PARTS = (1, 2, 3, 0)
EARLY = 4
SENT_AT = {1: 0, 2: 1024, 3: 2048, 0: 3072}
KEPT_AT = {1: 0, 2: 1024, 3: 2048}
HELD = (3072, 5120)
F32 = jnp.float32
BF16 = jnp.bfloat16
MIB = 1 << 20
SMALL = pl.CostEstimate(flops=1, bytes_accessed=1, transcendentals=0)

MATCH = ((1, 0, 3, 2), (3, 2, 1, 0))


def bits(v):
    b = lax.shift_right_logical(v, 1)
    return (v ^ b) & 1, b


def local_perm(dim):
    m = MATCH[dim % 2]
    if dim < 2:
        return [(z * 4 + x, z * 4 + m[x]) for z in range(4) for x in range(4)]
    return [(z * 4 + x, m[z] * 4 + x) for z in range(4) for x in range(4)]


def y_perm(k):
    return [(n, ((n // 2 + k) % 4) * 2 + n % 2) for n in range(8)]


CORE_PERM = [(n, n ^ 1) for n in range(8)]


def pad16(n):
    return -(-n // 16) * 16


def msg_rows(blocks):
    return blocks * 128 + pad16(blocks)


def params(mib):
    return pltpu.CompilerParams(vmem_limit_bytes=mib * MIB)


def vmem():
    return pl.BlockSpec(memory_space=pltpu.VMEM)


def quantize(m):
    top = jnp.max(jnp.abs(m), axis=0, keepdims=True) + 1e-06
    scale = top.astype(BF16).astype(F32)
    return (m * (1.0 / scale)).astype(BF16), scale


def encode(m):
    top = jnp.max(jnp.abs(m), axis=0, keepdims=True) + 1e-30
    scale = top.astype(BF16).astype(F32)
    e = jnp.exp2(jnp.abs(m) * (250.0 / scale) - 125.0)
    return jnp.where(m < 0, -e, e).astype(BF16), scale


def decode(code, scale):
    y = code.astype(F32)
    m = (jnp.log2(jnp.abs(y)) + 125.0) * (scale * (1.0 / 250.0))
    return jnp.where(y < 0, -m, m)


GROUPS = {"early": (0, EARLY), "late": (EARLY, RUNS)}


def aligned(v):
    return v if isinstance(v, int) else pl.multiple_of(v, 128)


def first_kernel(part, sent, group, fetch, *refs):
    order = [(part + s) % 4 for s in range(4)]
    if fetch and sent:
        tok, og, _, out, held, ogt, sc, sem, ogv = refs
    elif fetch:
        tok, ogt, _, out, held, sc, sem = refs
    else:
        held, ogt, _, out, sc = refs
    k0, k1 = GROUPS.get(group, (0, RUNS))
    me_l = lax.axis_index("local")
    ax, bx = bits(me_l & 3)
    az, bz = bits(lax.shift_right_logical(me_l, 2))

    def place_z(a, b):
        zb = b ^ bz
        return 2 * zb + (a ^ az ^ zb)

    if fetch:
        y = lax.shift_right_logical(lax.axis_index("node"), 1)
        copies = []
        if sent:
            copies.append(pltpu.make_async_copy(og, ogv, sem.at[0]))
        for p, at in (SENT_AT if sent else KEPT_AT).items():
            base = ((y + p) & 3) * 2048
            if p == 0:
                for i in range(4):
                    rows = pl.ds(i * TOK // 4, TOK // 4)
                    copies.append(pltpu.make_async_copy(
                        tok.at[rows, pl.ds(pl.multiple_of(base, 2048), 2048)],
                        held.at[rows, at:at + 2048],
                        sem.at[len(copies)],
                    ))
                continue
            for u in range(4 if p == 1 else 2):
                width = 128 if p == 1 else 256
                a, b = {1: (u & 1, u >> 1), 2: (sent, u), 3: (u, sent)}[p]
                lane = place_z(a, b) * 256 + ((sent ^ bx) * 128 if p == 1 else 0)
                for c in range(2):
                    to = at + c * 512 + u * width
                    copies.append(pltpu.make_async_copy(
                        tok.at[:, pl.ds(aligned(base + c * 1024 + lane), width)],
                        held.at[:, to:to + width],
                        sem.at[len(copies)],
                    ))
        for cp in copies:
            cp.start()
        if sent:
            copies.pop(0).wait()
            ogt[...] = ogv[...].T
        for cp in copies[:8]:
            cp.wait()

    for t in range(4):
        columns, places = [], []
        lo, hi = t & 1, t >> 1
        for x, a, b in {
            0: [(0, lo, hi), (1, lo, hi)], 1: [(sent, lo, hi)], 2: [(lo, sent, hi)], 3: [(lo, hi, sent)]
        }[part]:
            half = 512 if part else 1024
            lane = (SENT_AT if sent or not part else KEPT_AT)[part] + {
                0: place_z(a, b) * 256 + (x ^ bx) * 128,
                1: (a + 2 * b) * 128,
                2: b * 256 + (x ^ bx) * 128,
                3: a * 256 + (x ^ bx) * 128,
            }[part]
            t0 = held[:, pl.ds(aligned(lane), 128)]
            t1 = held[:, pl.ds(aligned(lane + half), 128)]
            swap = (x ^ bx ^ ax) == 1
            even = jnp.concatenate([t0[:, :64], t1[:, :64]], axis=1)
            odd = jnp.concatenate([t0[:, 64:], t1[:, 64:]], axis=1)
            for d in (sent,) if part == 0 else (0, 1):
                columns.append(jnp.where(swap, even, odd) if d else jnp.where(swap, odd, even))
                bit = (d, x, a, b)
                places.append(bit[order[1]] * 4 + bit[order[2]] * 2 + bit[order[3]])
        grad = jnp.dot(ogt[k0 * 128:k1 * 128, :], jnp.concatenate(columns, axis=1), preferred_element_type=F32)
        for k in range(k1 - k0):
            code, scale = quantize(grad[k * 128:(k + 1) * 128])
            for i, place in enumerate(places):
                block = place * (k1 - k0) + k
                out[block * 128:(block + 1) * 128, :] = code[:, i * 128:(i + 1) * 128]
                sc[block:block + 1, :] = scale[:, i * 128:(i + 1) * 128]
    out[8 * (k1 - k0) * 128:, :] = sc[...].astype(BF16)
    if fetch:
        for cp in copies[8:]:
            cp.wait()


def first_stage(part, sent, group, args, after, fetch=False):
    k0, k1 = GROUPS.get(group, (0, RUNS))
    blocks = 8 * (k1 - k0)
    out = [jax.ShapeDtypeStruct((msg_rows(blocks), 128), BF16)]
    scratch = [pltpu.VMEM((blocks, 128), F32)]
    anywhere = pl.BlockSpec(memory_space=pl.ANY)
    specs = [vmem()] * 2
    if fetch:
        out.append(jax.ShapeDtypeStruct((TOK, HELD[sent]), BF16))
        scratch.append(pltpu.SemaphoreType.DMA((21,)))
        specs = [anywhere] * 2 if sent else [anywhere, vmem()]
        if sent:
            out.append(jax.ShapeDtypeStruct((KV, TOK), BF16))
            scratch.append(pltpu.VMEM((TOK, KV), BF16))
    return pl.pallas_call(
        functools.partial(first_kernel, part, sent, group, fetch),
        out_shape=tuple(out),
        in_specs=specs + [anywhere],
        out_specs=tuple(vmem() for _ in out),
        scratch_shapes=scratch,
        compiler_params=params(20),
        cost_estimate=SMALL,
        name=f"grad_{'send' if sent else 'keep'}_{part}",
    )(*args, after)


def hold(message, *after):
    anywhere = pl.BlockSpec(memory_space=pl.ANY)
    return pl.pallas_call(
        lambda *refs: None,
        out_shape=jax.ShapeDtypeStruct(message.shape, message.dtype),
        in_specs=[anywhere] * (1 + len(after)),
        out_specs=anywhere,
        input_output_aliases={0: 0},
        compiler_params=params(1),
        cost_estimate=SMALL,
        name="hold",
    )(message, *after)


def early_sum_kernel(keep, recv, _, out, sc_keep, sc_recv, sc_out):
    sc_keep[...] = keep[8 * KV:, :].astype(F32)
    sc_recv[...] = recv[8 * EARLY * 128:, :].astype(F32)
    for t in range(4):
        for k in range(EARLY):
            block, there, to = (t + 4) * RUNS + k, (t + 4) * EARLY + k, t * EARLY + k
            m = keep[block * 128:(block + 1) * 128, :].astype(F32) * sc_keep[block:block + 1, :]
            m = m + recv[there * 128:(there + 1) * 128, :].astype(F32) * sc_recv[there:there + 1, :]
            out[to * 128:(to + 1) * 128, :], sc_out[to:to + 1, :] = encode(m)
    out[4 * EARLY * 128:, :] = sc_out[...].astype(BF16)


def early_sum_stage(keep, recv, after):
    return pl.pallas_call(
        early_sum_kernel,
        out_shape=jax.ShapeDtypeStruct((msg_rows(4 * EARLY), 128), BF16),
        in_specs=[vmem(), vmem(), pl.BlockSpec(memory_space=pl.ANY)],
        out_specs=vmem(),
        scratch_shapes=[
            pltpu.VMEM((8 * RUNS, 128), F32),
            pltpu.VMEM((8 * EARLY, 128), F32),
            pltpu.VMEM((4 * EARLY, 128), F32),
        ],
        compiler_params=params(16),
        cost_estimate=SMALL,
        name="sum_early",
    )(keep, recv, after)


def sum_kernel(tiles, send, n, *refs):
    half = tiles // 2
    keep, recvs = refs[0], refs[1:1 + n]
    out, sc_keep, sc_recv, sc_out = refs[2 + n:]
    coded = tiles < 8
    counts = [EARLY, RUNS - EARLY] if n == 2 else [RUNS]
    ready = send and n == 2
    for j, r in enumerate(recvs):
        blocks = counts[j] * (half if ready and j == 0 else tiles)
        sc_recv[j, :blocks, :] = r[blocks * 128:blocks * 128 + pad16(blocks), :].astype(F32)[:blocks]
    if not coded:
        sc_keep[...] = keep[tiles * RUNS * 128:, :].astype(F32)

    def body(t, _):
        source = t + half if send else t
        k = 0
        for j, r in enumerate(recvs):
            for i in range(counts[j]):
                to = t * RUNS + k
                if ready and j == 0:
                    there = t * counts[0] + i
                    out[pl.ds(aligned(to * 128), 128), :] = r[pl.ds(aligned(there * 128), 128), :]
                    sc_out[pl.ds(to, 1), :] = sc_recv[0, pl.ds(there, 1), :]
                    k += 1
                    continue
                block = source * RUNS + k
                kept = keep[pl.ds(aligned(block * 128), 128), :]
                there = source * counts[j] + i
                came = r[pl.ds(aligned(there * 128), 128), :]
                scale = sc_recv[j, pl.ds(there, 1), :]
                if coded:
                    m = kept + decode(came, scale)
                else:
                    m = kept.astype(F32) * sc_keep[pl.ds(block, 1), :] + came.astype(F32) * scale
                if send:
                    m, scale = encode(m)
                    sc_out[pl.ds(to, 1), :] = scale
                out[pl.ds(aligned(to * 128), 128), :] = m
                k += 1
        return 0

    if half == 1:
        body(0, 0)
    else:
        lax.fori_loop(0, half, body, 0)
    if send:
        out[half * RUNS * 128:, :] = sc_out[...].astype(BF16)


def sum_stage(keep, recvs, tiles, send, after):
    n = len(recvs)
    half = tiles // 2 * RUNS
    return pl.pallas_call(
        functools.partial(sum_kernel, tiles, send, n),
        out_shape=jax.ShapeDtypeStruct((msg_rows(half), 128), BF16) if send else jax.ShapeDtypeStruct((half * 128, 128), F32),
        in_specs=[vmem()] * (1 + n) + [pl.BlockSpec(memory_space=pl.ANY)],
        out_specs=vmem(),
        scratch_shapes=[
            pltpu.VMEM((pad16(tiles * RUNS), 128), F32),
            pltpu.VMEM((n, pad16(tiles * RUNS), 128), F32),
            pltpu.VMEM((pad16(half), 128), F32),
        ],
        compiler_params=params(16),
        cost_estimate=SMALL,
        name=f"sum_{'send' if send else 'keep'}_{tiles}",
    )(keep, *recvs, after)


def pack(lo, hi, core):
    first = jnp.concatenate([lo[:, :64], hi[:, :64]], axis=1)
    second = jnp.concatenate([lo[:, 64:], hi[:, 64:]], axis=1)
    return jnp.where(core == 0, first, second), jnp.where(core == 0, second, first)


def requantize_kernel(keep, recv, _, mine, other, sc):
    core = lax.axis_index("node") & 1
    sc[0] = recv[KV:KV + 16, :].astype(F32)
    for k in range(RUNS // 2):
        made = []
        for j in (k, k + RUNS // 2):
            rows = slice(j * 128, (j + 1) * 128)
            made.append(quantize(keep[rows, :] + decode(recv[rows, :], sc[0, j:j + 1, :])))
        codes = pack(made[0][0], made[1][0], core)
        scales = pack(made[0][1], made[1][1], core)
        for i, out in enumerate((mine, other)):
            out[k * 128:(k + 1) * 128, :] = codes[i]
            sc[1 + i, k:k + 1, :] = scales[i]
    mine[HALF:, :] = sc[1].astype(BF16)
    other[HALF:, :] = sc[2].astype(BF16)


def requantize_stage(keep, recv, after):
    out = jax.ShapeDtypeStruct((HALF + 16, 128), BF16)
    return pl.pallas_call(
        requantize_kernel,
        out_shape=(out, out),
        in_specs=[vmem(), vmem(), pl.BlockSpec(memory_space=pl.ANY)],
        out_specs=(vmem(), vmem()),
        scratch_shapes=[pltpu.VMEM((3, 16, 128), F32)],
        compiler_params=params(8),
        cost_estimate=SMALL,
        name="requantize",
    )(keep, recv, after)


def core_sum_kernel(coded, mine, recv, _, out, sc):
    sc[0] = mine[HALF:, :].astype(F32)
    sc[1] = recv[HALF:, :].astype(F32)
    for k in range(RUNS // 2):
        rows = slice(k * 128, (k + 1) * 128)
        m = mine[rows, :].astype(F32) * sc[0, k:k + 1, :] + recv[rows, :].astype(F32) * sc[1, k:k + 1, :]
        if coded:
            m, sc[2, k:k + 1, :] = encode(m)
        out[rows, :] = m
    if coded:
        out[HALF:, :] = sc[2].astype(BF16)


def core_sum_stage(mine, recv, coded, after):
    out = jax.ShapeDtypeStruct((HALF + 16, 128), BF16) if coded else jax.ShapeDtypeStruct((HALF, 128), F32)
    return pl.pallas_call(
        functools.partial(core_sum_kernel, coded),
        out_shape=out,
        in_specs=[vmem(), vmem(), pl.BlockSpec(memory_space=pl.ANY)],
        out_specs=vmem(),
        scratch_shapes=[pltpu.VMEM((3, 16, 128), F32)],
        compiler_params=params(8),
        cost_estimate=SMALL,
        name="core_sum",
    )(mine, recv, after)


def adam_rule(grad, master, moment, second):
    m = 0.9 * moment + 0.1 * grad
    s = 0.95 * second + 0.05 * grad * grad
    update = m / (1.0 - 0.9**10) / (jnp.sqrt(s / (1.0 - 0.95**10)) + 1e-08) + 0.1 * master
    return master - 0.05 * update, m, s


def weight_kernel(own, a, b, c, master, moment, second, weight, grad, sc, g):
    for i, r in enumerate((a, b, c)):
        sc[i] = r[HALF:, :].astype(F32)
    for k in range(RUNS // 2):
        rows = slice(k * 128, (k + 1) * 128)
        m = own[rows, :]
        for i, r in enumerate((a, b, c)):
            m = m + decode(r[rows, :], sc[i, k:k + 1, :])
        g[rows, :] = m
    t = g[...].T
    whole = jnp.concatenate([t[:64], t[64:]], axis=1)
    grad[...] = whole
    weight[...] = adam_rule(whole, master[...], moment[...], second[...])[0].astype(BF16)


def weight_stage(own, others, master, moment, second):
    return pl.pallas_call(
        weight_kernel,
        out_shape=(jax.ShapeDtypeStruct((64, KV), BF16), jax.ShapeDtypeStruct((64, KV), F32)),
        in_specs=[vmem()] * 7,
        out_specs=(vmem(),) * 2,
        scratch_shapes=[pltpu.VMEM((3, 16, 128), F32), pltpu.VMEM((HALF, 128), F32)],
        compiler_params=params(8),
        cost_estimate=SMALL,
        name="adam_weight",
    )(own, *others, master, moment, second)


def adam_kernel(grad, master, moment, second, new_master, new_moment, new_second, mark):
    mark[...] = jnp.zeros_like(mark)
    new_master[...], new_moment[...], new_second[...] = adam_rule(grad[...], master[...], moment[...], second[...])


def adam_stage(*arrays):
    f = jax.ShapeDtypeStruct((64, KV), F32)
    return pl.pallas_call(
        adam_kernel,
        out_shape=(f, f, f, jax.ShapeDtypeStruct((8, 128), F32)),
        in_specs=[vmem()] * 4,
        out_specs=(vmem(),) * 4,
        compiler_params=params(8),
        cost_estimate=SMALL,
        name="adam",
    )(*arrays)


def gather_kernel(*refs):
    me_n = lax.axis_index("node")
    y = lax.shift_right_logical(me_n, 1)
    core = me_n & 1
    weight = refs[8]
    for k in range(4):
        src = ((y - k) & 3) * 2
        weight[src + core] = refs[k][...]
        weight[src + 1 - core] = refs[4 + k][...]


def gather_stage(weights):
    return pl.pallas_call(
        gather_kernel,
        out_shape=jax.ShapeDtypeStruct((8, 64, KV), BF16),
        in_specs=[vmem()] * 8,
        out_specs=vmem(),
        compiler_params=params(8),
        cost_estimate=SMALL,
        name="gather",
    )(*weights)


def local(tokens, out_grads, master, moment, second):
    tokens = pltpu.with_memory_space_constraint(tokens, pltpu.HBM)
    out_grads = pltpu.with_memory_space_constraint(out_grads, pltpu.HBM)
    keep, recv, early, late = {}, {}, {}, {}
    after, args = out_grads, (tokens, out_grads)
    for i, p in enumerate(PARTS):
        after, *more = first_stage(p, 1, "early", args, after, i == 0)
        args = tuple(more) or args
        early[p] = lax.ppermute(after, "local", local_perm(p))
    for p in PARTS:
        after, = first_stage(p, 1, "late", args, after)
        late[p] = after
    for p in PARTS:
        after = hold(late[p], early[p], *(late[q] for q in PARTS[3:] if q != p))
        recv[p] = [early[p], lax.ppermute(after, "local", local_perm(p))]
    held, ogt = args
    for i, p in enumerate(PARTS):
        after, *more = first_stage(p, 0, None, (tokens if i == 0 else args[0] if p == 0 else held, ogt), after, i == 0)
        held, = more or [held]
        keep[p] = after
    ready = {}
    for p in PARTS:
        ready[p] = after = early_sum_stage(keep[p], early[p], after)
    for step, tiles in ((1, 8), (2, 4), (3, 2)):
        arrived = dict(recv)
        for p in PARTS:
            came = [ready[p], arrived[p][1]] if step == 1 else arrived[p]
            after = sum_stage(keep[p], came, tiles, True, after)
            recv[p] = [lax.ppermute(after, "local", local_perm((p + step) % 4))]
        for p in PARTS:
            after = keep[p] = sum_stage(keep[p], arrived[p], tiles, False, after)
    mine, other, parts = {}, {}, {}
    one, two, three, own = PARTS
    for p, summed in ((one, None), (two, one), (three, two), (own, three), (None, own)):
        if p is not None:
            mine[p], other[p] = requantize_stage(keep[p], recv[p][0], after)
            after = mine[p]
            other[p] = lax.ppermute(other[p], "node", CORE_PERM)
        if summed is not None:
            after = core_sum_stage(mine[summed], other[summed], summed > 0, after)
            parts[summed] = lax.ppermute(after, "node", y_perm(summed)) if summed else after
    w, grad = weight_stage(parts[0], [parts[p] for p in (1, 2, 3)], master, moment, second)
    own = [w] + [lax.ppermute(w, "node", y_perm(k)) for k in (1, 2, 3)]
    *new, mark = adam_stage(grad, master, moment, second)
    own[3] = hold(own[3], mark)
    own += [lax.ppermute(v, "node", CORE_PERM) for v in own]
    return (*new, gather_stage(own))


def solution(mesh):
    rows = P(("node", "local"), None)
    return jax.shard_map(
        local,
        mesh=mesh,
        in_specs=(rows,) * 5,
        out_specs=(rows, rows, rows, P(None, "local", None)),
        check_vma=False,
    )
```

```python
import functools

import jax
import jax.numpy as jnp
from jax import lax
from jax.experimental import pallas as pl
from jax.experimental.pallas import tpu as pltpu
from jax.sharding import PartitionSpec as P

D = 8192
KV = 1024
TOK = 768
RUNS = KV // 128
HALF = KV // 2
PARTS = (1, 2, 3, 0)
EARLY = 4
SENT_AT = {1: 0, 2: 1024, 3: 2048, 0: 3072}
KEPT_AT = {1: 0, 2: 1024, 3: 2048}
HELD = (3072, 5120)
F32 = jnp.float32
BF16 = jnp.bfloat16
MIB = 1 << 20
SMALL = pl.CostEstimate(flops=1, bytes_accessed=1, transcendentals=0)

MATCH = ((1, 0, 3, 2), (3, 2, 1, 0))


def bits(v):
    b = lax.shift_right_logical(v, 1)
    return (v ^ b) & 1, b


def local_perm(dim):
    m = MATCH[dim % 2]
    if dim < 2:
        return [(z * 4 + x, z * 4 + m[x]) for z in range(4) for x in range(4)]
    return [(z * 4 + x, m[z] * 4 + x) for z in range(4) for x in range(4)]


def y_perm(k):
    return [(n, ((n // 2 + k) % 4) * 2 + n % 2) for n in range(8)]


CORE_PERM = [(n, n ^ 1) for n in range(8)]


def pad16(n):
    return -(-n // 16) * 16


def msg_rows(blocks):
    return blocks * 128 + pad16(blocks)


def params(mib):
    return pltpu.CompilerParams(vmem_limit_bytes=mib * MIB)


def vmem():
    return pl.BlockSpec(memory_space=pltpu.VMEM)


def quantize(m):
    top = jnp.max(jnp.abs(m), axis=0, keepdims=True) + 1e-06
    scale = top.astype(BF16).astype(F32)
    return (m * (1.0 / scale)).astype(BF16), scale


def encode(m):
    top = jnp.max(jnp.abs(m), axis=0, keepdims=True) + 1e-30
    scale = top.astype(BF16).astype(F32)
    e = jnp.exp2(jnp.abs(m) * (250.0 / scale) - 125.0)
    return jnp.where(m < 0, -e, e).astype(BF16), scale


def decode(code, scale):
    y = code.astype(F32)
    m = (jnp.log2(jnp.abs(y)) + 125.0) * (scale * (1.0 / 250.0))
    return jnp.where(y < 0, -m, m)


GROUPS = {"early": (0, EARLY), "late": (EARLY, RUNS)}


def aligned(v):
    return v if isinstance(v, int) else pl.multiple_of(v, 128)


def first_kernel(part, sent, group, fetch, *refs):
    order = [(part + s) % 4 for s in range(4)]
    if fetch and sent:
        tok, og, _, out, held, ogt, sc, sem, ogv = refs
    elif fetch:
        tok, ogt, _, out, held, sc, sem = refs
    else:
        held, ogt, _, out, sc = refs
    k0, k1 = GROUPS.get(group, (0, RUNS))
    me_l = lax.axis_index("local")
    ax, bx = bits(me_l & 3)
    az, bz = bits(lax.shift_right_logical(me_l, 2))

    def place_z(a, b):
        zb = b ^ bz
        return 2 * zb + (a ^ az ^ zb)

    if fetch:
        y = lax.shift_right_logical(lax.axis_index("node"), 1)
        copies = []
        if sent:
            copies.append(pltpu.make_async_copy(og, ogv, sem.at[0]))
        for p, at in (SENT_AT if sent else KEPT_AT).items():
            base = ((y + p) & 3) * 2048
            if p == 0:
                for i in range(4):
                    rows = pl.ds(i * TOK // 4, TOK // 4)
                    copies.append(pltpu.make_async_copy(
                        tok.at[rows, pl.ds(pl.multiple_of(base, 2048), 2048)],
                        held.at[rows, at:at + 2048],
                        sem.at[len(copies)],
                    ))
                continue
            for u in range(4 if p == 1 else 2):
                width = 128 if p == 1 else 256
                a, b = {1: (u & 1, u >> 1), 2: (sent, u), 3: (u, sent)}[p]
                lane = place_z(a, b) * 256 + ((sent ^ bx) * 128 if p == 1 else 0)
                for c in range(2):
                    to = at + c * 512 + u * width
                    copies.append(pltpu.make_async_copy(
                        tok.at[:, pl.ds(aligned(base + c * 1024 + lane), width)],
                        held.at[:, to:to + width],
                        sem.at[len(copies)],
                    ))
        for cp in copies:
            cp.start()
        if sent:
            copies.pop(0).wait()
            ogt[...] = ogv[...].T
        for cp in copies[:8]:
            cp.wait()

    for t in range(4):
        columns, places = [], []
        lo, hi = t & 1, t >> 1
        for x, a, b in {
            0: [(0, lo, hi), (1, lo, hi)], 1: [(sent, lo, hi)], 2: [(lo, sent, hi)], 3: [(lo, hi, sent)]
        }[part]:
            half = 512 if part else 1024
            lane = (SENT_AT if sent or not part else KEPT_AT)[part] + {
                0: place_z(a, b) * 256 + (x ^ bx) * 128,
                1: (a + 2 * b) * 128,
                2: b * 256 + (x ^ bx) * 128,
                3: a * 256 + (x ^ bx) * 128,
            }[part]
            t0 = held[:, pl.ds(aligned(lane), 128)]
            t1 = held[:, pl.ds(aligned(lane + half), 128)]
            swap = (x ^ bx ^ ax) == 1
            even = jnp.concatenate([t0[:, :64], t1[:, :64]], axis=1)
            odd = jnp.concatenate([t0[:, 64:], t1[:, 64:]], axis=1)
            for d in (sent,) if part == 0 else (0, 1):
                columns.append(jnp.where(swap, even, odd) if d else jnp.where(swap, odd, even))
                bit = (d, x, a, b)
                places.append(bit[order[1]] * 4 + bit[order[2]] * 2 + bit[order[3]])
        grad = jnp.dot(ogt[k0 * 128:k1 * 128, :], jnp.concatenate(columns, axis=1), preferred_element_type=F32)
        for k in range(k1 - k0):
            code, scale = quantize(grad[k * 128:(k + 1) * 128])
            for i, place in enumerate(places):
                block = place * (k1 - k0) + k
                out[block * 128:(block + 1) * 128, :] = code[:, i * 128:(i + 1) * 128]
                sc[block:block + 1, :] = scale[:, i * 128:(i + 1) * 128]
    out[8 * (k1 - k0) * 128:, :] = sc[...].astype(BF16)
    if fetch:
        for cp in copies[8:]:
            cp.wait()


def first_stage(part, sent, group, args, after, fetch=False):
    k0, k1 = GROUPS.get(group, (0, RUNS))
    blocks = 8 * (k1 - k0)
    out = [jax.ShapeDtypeStruct((msg_rows(blocks), 128), BF16)]
    scratch = [pltpu.VMEM((blocks, 128), F32)]
    anywhere = pl.BlockSpec(memory_space=pl.ANY)
    specs = [vmem()] * 2
    if fetch:
        out.append(jax.ShapeDtypeStruct((TOK, HELD[sent]), BF16))
        scratch.append(pltpu.SemaphoreType.DMA((21,)))
        specs = [anywhere] * 2 if sent else [anywhere, vmem()]
        if sent:
            out.append(jax.ShapeDtypeStruct((KV, TOK), BF16))
            scratch.append(pltpu.VMEM((TOK, KV), BF16))
    return pl.pallas_call(
        functools.partial(first_kernel, part, sent, group, fetch),
        out_shape=tuple(out),
        in_specs=specs + [anywhere],
        out_specs=tuple(vmem() for _ in out),
        scratch_shapes=scratch,
        compiler_params=params(20),
        cost_estimate=SMALL,
        name=f"grad_{'send' if sent else 'keep'}_{part}",
    )(*args, after)


def hold(message, *after):
    anywhere = pl.BlockSpec(memory_space=pl.ANY)
    return pl.pallas_call(
        lambda *refs: None,
        out_shape=jax.ShapeDtypeStruct(message.shape, message.dtype),
        in_specs=[anywhere] * (1 + len(after)),
        out_specs=anywhere,
        input_output_aliases={0: 0},
        compiler_params=params(1),
        cost_estimate=SMALL,
        name="hold",
    )(message, *after)


def early_sum_kernel(keep, recv, _, out, sc_keep, sc_recv, sc_out):
    sc_keep[...] = keep[8 * KV:, :].astype(F32)
    sc_recv[...] = recv[8 * EARLY * 128:, :].astype(F32)

    def body(t, _):
        for k in range(EARLY):
            block, there, to = (t + 4) * RUNS + k, (t + 4) * EARLY + k, t * EARLY + k
            m = keep[pl.ds(aligned(block * 128), 128), :].astype(F32) * sc_keep[pl.ds(block, 1), :]
            m = m + recv[pl.ds(aligned(there * 128), 128), :].astype(F32) * sc_recv[pl.ds(there, 1), :]
            code, sc_out[pl.ds(to, 1), :] = encode(m)
            out[pl.ds(aligned(to * 128), 128), :] = code
        return 0

    lax.fori_loop(0, 4, body, 0)
    out[4 * EARLY * 128:, :] = sc_out[...].astype(BF16)


def early_sum_stage(keep, recv, after):
    return pl.pallas_call(
        early_sum_kernel,
        out_shape=jax.ShapeDtypeStruct((msg_rows(4 * EARLY), 128), BF16),
        in_specs=[vmem(), vmem(), pl.BlockSpec(memory_space=pl.ANY)],
        out_specs=vmem(),
        scratch_shapes=[
            pltpu.VMEM((8 * RUNS, 128), F32),
            pltpu.VMEM((8 * EARLY, 128), F32),
            pltpu.VMEM((4 * EARLY, 128), F32),
        ],
        compiler_params=params(16),
        cost_estimate=SMALL,
        name="sum_early",
    )(keep, recv, after)


def sum_kernel(tiles, send, n, *refs):
    half = tiles // 2
    keep, recvs = refs[0], refs[1:1 + n]
    out, sc_keep, sc_recv, sc_out = refs[2 + n:]
    coded = tiles < 8
    counts = [EARLY, RUNS - EARLY] if n == 2 else [RUNS]
    ready = send and n == 2
    for j, r in enumerate(recvs):
        blocks = counts[j] * (half if ready and j == 0 else tiles)
        sc_recv[j, :blocks, :] = r[blocks * 128:blocks * 128 + pad16(blocks), :].astype(F32)[:blocks]
    if not coded:
        sc_keep[...] = keep[tiles * RUNS * 128:, :].astype(F32)

    def body(t, _):
        source = t + half if send else t
        k = 0
        for j, r in enumerate(recvs):
            for i in range(counts[j]):
                to = t * RUNS + k
                if ready and j == 0:
                    there = t * counts[0] + i
                    out[pl.ds(aligned(to * 128), 128), :] = r[pl.ds(aligned(there * 128), 128), :]
                    sc_out[pl.ds(to, 1), :] = sc_recv[0, pl.ds(there, 1), :]
                    k += 1
                    continue
                block = source * RUNS + k
                kept = keep[pl.ds(aligned(block * 128), 128), :]
                there = source * counts[j] + i
                came = r[pl.ds(aligned(there * 128), 128), :]
                scale = sc_recv[j, pl.ds(there, 1), :]
                if coded:
                    m = kept + decode(came, scale)
                else:
                    m = kept.astype(F32) * sc_keep[pl.ds(block, 1), :] + came.astype(F32) * scale
                if send:
                    m, scale = encode(m)
                    sc_out[pl.ds(to, 1), :] = scale
                out[pl.ds(aligned(to * 128), 128), :] = m
                k += 1
        return 0

    if half == 1:
        body(0, 0)
    else:
        lax.fori_loop(0, half, body, 0)
    if send:
        out[half * RUNS * 128:, :] = sc_out[...].astype(BF16)


def sum_stage(keep, recvs, tiles, send, after):
    n = len(recvs)
    half = tiles // 2 * RUNS
    return pl.pallas_call(
        functools.partial(sum_kernel, tiles, send, n),
        out_shape=jax.ShapeDtypeStruct((msg_rows(half), 128), BF16) if send else jax.ShapeDtypeStruct((half * 128, 128), F32),
        in_specs=[vmem()] * (1 + n) + [pl.BlockSpec(memory_space=pl.ANY)],
        out_specs=vmem(),
        scratch_shapes=[
            pltpu.VMEM((pad16(tiles * RUNS), 128), F32),
            pltpu.VMEM((n, pad16(tiles * RUNS), 128), F32),
            pltpu.VMEM((pad16(half), 128), F32),
        ],
        compiler_params=params(16),
        cost_estimate=SMALL,
        name=f"sum_{'send' if send else 'keep'}_{tiles}",
    )(keep, *recvs, after)


def pack(lo, hi, core):
    first = jnp.concatenate([lo[:, :64], hi[:, :64]], axis=1)
    second = jnp.concatenate([lo[:, 64:], hi[:, 64:]], axis=1)
    return jnp.where(core == 0, first, second), jnp.where(core == 0, second, first)


def requantize_kernel(keep, recv, _, mine, other, sc):
    core = lax.axis_index("node") & 1
    sc[0] = recv[KV:KV + 16, :].astype(F32)
    for k in range(RUNS // 2):
        made = []
        for j in (k, k + RUNS // 2):
            rows = slice(j * 128, (j + 1) * 128)
            made.append(quantize(keep[rows, :] + decode(recv[rows, :], sc[0, j:j + 1, :])))
        codes = pack(made[0][0], made[1][0], core)
        scales = pack(made[0][1], made[1][1], core)
        for i, out in enumerate((mine, other)):
            out[k * 128:(k + 1) * 128, :] = codes[i]
            sc[1 + i, k:k + 1, :] = scales[i]
    mine[HALF:, :] = sc[1].astype(BF16)
    other[HALF:, :] = sc[2].astype(BF16)


def requantize_stage(keep, recv, after):
    out = jax.ShapeDtypeStruct((HALF + 16, 128), BF16)
    return pl.pallas_call(
        requantize_kernel,
        out_shape=(out, out),
        in_specs=[vmem(), vmem(), pl.BlockSpec(memory_space=pl.ANY)],
        out_specs=(vmem(), vmem()),
        scratch_shapes=[pltpu.VMEM((3, 16, 128), F32)],
        compiler_params=params(8),
        cost_estimate=SMALL,
        name="requantize",
    )(keep, recv, after)


def core_sum_kernel(coded, mine, recv, _, out, sc):
    sc[0] = mine[HALF:, :].astype(F32)
    sc[1] = recv[HALF:, :].astype(F32)
    for k in range(RUNS // 2):
        rows = slice(k * 128, (k + 1) * 128)
        m = mine[rows, :].astype(F32) * sc[0, k:k + 1, :] + recv[rows, :].astype(F32) * sc[1, k:k + 1, :]
        if coded:
            m, sc[2, k:k + 1, :] = encode(m)
        out[rows, :] = m
    if coded:
        out[HALF:, :] = sc[2].astype(BF16)


def core_sum_stage(mine, recv, coded, after):
    out = jax.ShapeDtypeStruct((HALF + 16, 128), BF16) if coded else jax.ShapeDtypeStruct((HALF, 128), F32)
    return pl.pallas_call(
        functools.partial(core_sum_kernel, coded),
        out_shape=out,
        in_specs=[vmem(), vmem(), pl.BlockSpec(memory_space=pl.ANY)],
        out_specs=vmem(),
        scratch_shapes=[pltpu.VMEM((3, 16, 128), F32)],
        compiler_params=params(8),
        cost_estimate=SMALL,
        name="core_sum",
    )(mine, recv, after)


def adam_rule(grad, master, moment, second):
    m = 0.9 * moment + 0.1 * grad
    s = 0.95 * second + 0.05 * grad * grad
    update = m / (1.0 - 0.9**10) / (jnp.sqrt(s / (1.0 - 0.95**10)) + 1e-08) + 0.1 * master
    return master - 0.05 * update, m, s


def weight_kernel(own, a, b, c, master, moment, second, weight, grad, sc, g):
    for i, r in enumerate((a, b, c)):
        sc[i] = r[HALF:, :].astype(F32)
    for k in range(RUNS // 2):
        rows = slice(k * 128, (k + 1) * 128)
        m = own[rows, :]
        for i, r in enumerate((a, b, c)):
            m = m + decode(r[rows, :], sc[i, k:k + 1, :])
        g[rows, :] = m
    t = g[...].T
    whole = jnp.concatenate([t[:64], t[64:]], axis=1)
    grad[...] = whole
    weight[...] = adam_rule(whole, master[...], moment[...], second[...])[0].astype(BF16)


def weight_stage(own, others, master, moment, second):
    return pl.pallas_call(
        weight_kernel,
        out_shape=(jax.ShapeDtypeStruct((64, KV), BF16), jax.ShapeDtypeStruct((64, KV), F32)),
        in_specs=[vmem()] * 7,
        out_specs=(vmem(),) * 2,
        scratch_shapes=[pltpu.VMEM((3, 16, 128), F32), pltpu.VMEM((HALF, 128), F32)],
        compiler_params=params(8),
        cost_estimate=SMALL,
        name="adam_weight",
    )(own, *others, master, moment, second)


def adam_kernel(grad, master, moment, second, new_master, new_moment, new_second, mark):
    mark[...] = jnp.zeros_like(mark)
    new_master[...], new_moment[...], new_second[...] = adam_rule(grad[...], master[...], moment[...], second[...])


def adam_stage(*arrays):
    f = jax.ShapeDtypeStruct((64, KV), F32)
    return pl.pallas_call(
        adam_kernel,
        out_shape=(f, f, f, jax.ShapeDtypeStruct((8, 128), F32)),
        in_specs=[vmem()] * 4,
        out_specs=(vmem(),) * 4,
        compiler_params=params(8),
        cost_estimate=SMALL,
        name="adam",
    )(*arrays)


def gather_kernel(*refs):
    me_n = lax.axis_index("node")
    y = lax.shift_right_logical(me_n, 1)
    core = me_n & 1
    weight = refs[8]
    for k in range(4):
        src = ((y - k) & 3) * 2
        weight[src + core] = refs[k][...]
        weight[src + 1 - core] = refs[4 + k][...]


def gather_stage(weights):
    return pl.pallas_call(
        gather_kernel,
        out_shape=jax.ShapeDtypeStruct((8, 64, KV), BF16),
        in_specs=[vmem()] * 8,
        out_specs=vmem(),
        compiler_params=params(8),
        cost_estimate=SMALL,
        name="gather",
    )(*weights)


def local(tokens, out_grads, master, moment, second):
    tokens = pltpu.with_memory_space_constraint(tokens, pltpu.HBM)
    out_grads = pltpu.with_memory_space_constraint(out_grads, pltpu.HBM)
    keep, recv, early, late = {}, {}, {}, {}
    after, args = out_grads, (tokens, out_grads)
    for i, p in enumerate(PARTS):
        after, *more = first_stage(p, 1, "early", args, after, i == 0)
        args = tuple(more) or args
        early[p] = lax.ppermute(after, "local", local_perm(p))
    for p in PARTS:
        after, = first_stage(p, 1, "late", args, after)
        late[p] = after
    for p in PARTS:
        after = hold(late[p], early[p], *(late[q] for q in PARTS[3:] if q != p))
        recv[p] = [early[p], lax.ppermute(after, "local", local_perm(p))]
    held, ogt = args
    for i, p in enumerate(PARTS):
        after, *more = first_stage(p, 0, None, (tokens if i == 0 else args[0] if p == 0 else held, ogt), after, i == 0)
        held, = more or [held]
        keep[p] = after
    ready = {}
    for p in PARTS:
        ready[p] = after = early_sum_stage(keep[p], early[p], after)
    for step, tiles in ((1, 8), (2, 4), (3, 2)):
        arrived = dict(recv)
        for p in PARTS:
            came = [ready[p], arrived[p][1]] if step == 1 else arrived[p]
            after = sum_stage(keep[p], came, tiles, True, after)
            recv[p] = [lax.ppermute(after, "local", local_perm((p + step) % 4))]
        for p in PARTS:
            after = keep[p] = sum_stage(keep[p], arrived[p], tiles, False, after)
    mine, other, parts = {}, {}, {}
    one, two, three, own = PARTS
    for p, summed in ((one, None), (two, one), (three, two), (own, three), (None, own)):
        if p is not None:
            mine[p], other[p] = requantize_stage(keep[p], recv[p][0], after)
            after = mine[p]
            other[p] = lax.ppermute(other[p], "node", CORE_PERM)
        if summed is not None:
            after = core_sum_stage(mine[summed], other[summed], summed > 0, after)
            parts[summed] = lax.ppermute(after, "node", y_perm(summed)) if summed else after
    w, grad = weight_stage(parts[0], [parts[p] for p in (1, 2, 3)], master, moment, second)
    own = [w] + [lax.ppermute(w, "node", y_perm(k)) for k in (1, 2, 3)]
    *new, mark = adam_stage(grad, master, moment, second)
    own[3] = hold(own[3], mark)
    own += [lax.ppermute(v, "node", CORE_PERM) for v in own]
    return (*new, gather_stage(own))


def solution(mesh):
    rows = P(("node", "local"), None)
    return jax.shard_map(
        local,
        mesh=mesh,
        in_specs=(rows,) * 5,
        out_specs=(rows, rows, rows, P(None, "local", None)),
        check_vma=False,
    )
```
